32 devices in a mesh: batch: 16 (over z, y, core), heads: 2 (over x).
Axes of the slice: x: 2, y: 2, z: 4, core: 2. Of those that a mesh axis runs over, the one named last changes fastest.
Arguments:
- token_ids: int32 [128, 2, 5], P('batch'), may hold values from 0 to 65535
- accepted: int32 [128], P('batch'), may hold values from 0 to 4
- lengths: int32 [128], P('batch'), may hold values from 128 to 512
- queries: bfloat16 [128, 2, 5, 4096], P('batch', None, None, 'heads'), may hold values from -8 to 8
- new_kv: bfloat16 [128, 2, 2, 5, 1024], P('batch', None, None, None, 'heads'), may hold values from -4 to 4
- cache_kv: bfloat16 [128, 2, 512, 1024], P('batch', None, None, 'heads'), may hold values from -8 to 8
- table: bfloat16 [65536, 8192], P('heads', 'batch'), may hold values from -6 to 6
- w_out: bfloat16 [4096, 8192], P('heads', 'batch'), may hold values from -0.1875 to 0.1875
- gain: float32 [8192], P('batch'), may hold values from 0.25 to 1.75
- w_feat: bfloat16 [8192, 8192], P('batch', 'heads'), may hold values from -0.0625 to 0.0625
- w_emb: bfloat16 [8192, 8192], P('batch', 'heads'), may hold values from -0.0625 to 0.0625
Outputs:
- verified_hidden: bfloat16 [1280, 8192], P(None, 'batch')
- draft_feat: bfloat16 [128, 2, 5, 8192], P('batch', None, None, 'heads')
The draws below stay inside these ranges and needn't reach their ends.
All inputs are finite; a program needn't handle non-finite values.
Results may differ from the reference program's by a relative error of at most 0.0043.
Values may be sent and summed in bfloat16 or wider, within the bound.
A program may use at most 128 MiB of HBM per device.

```python
import jax
import jax.numpy as jnp
from jax import lax

D = 8192
HQ = 32
KV = 8
HD = 128
VOCAB = 65536
DRAFT = 4
CTX = 512
ROWS = 128


def draw_cache_kv(key, part):
    noise = jnp.clip(0.5 * jax.random.normal(jax.random.fold_in(key, 2), (ROWS, 2, CTX, KV * HD), jnp.float32), -4.0, 4.0)
    return noise.astype(jnp.bfloat16)


def draw_queries(key, part):
    noise = jnp.clip(0.5 * jax.random.normal(jax.random.fold_in(key, 1), (ROWS, 2, DRAFT + 1, HQ * HD), jnp.float32), -4.0, 4.0)
    return noise.astype(jnp.bfloat16)


def with_ends(values, rng, least, top_value):
    index_at = [jax.random.randint(jax.random.fold_in(rng, axis), (), 0, length) for axis, length in enumerate(values.shape)]
    widest = values.shape.index(max(values.shape))
    next_to = index_at[:widest] + [(index_at[widest] + 1) % values.shape[widest]] + index_at[widest + 1:]
    return values.at[tuple(index_at)].set(least).at[tuple(next_to)].set(top_value)


def steps_of(key, shape, cuts, least, high):
    def one(position, shards_of):
        steps = jax.random.uniform(jax.random.fold_in(jax.random.fold_in(key, 6), position), (shards_of,), jnp.float32, least / len(cuts), high / len(cuts))
        return jnp.repeat(jnp.exp(steps), shape[position] // shards_of).reshape((-1,) + (1,) * (len(shape) - position - 1))

    level = one(*cuts[0])
    for cut in cuts[1:]:
        level = level * one(*cut)
    return level


def gaussian(own_key, shape, spread, limit, pieces=(), kind=jnp.bfloat16):
    loudness = steps_of(own_key, shape, pieces, -0.22, 0.18) if pieces else 1.0
    values = jax.random.normal(own_key, shape, jnp.float32) * spread * loudness
    return jnp.minimum(jnp.maximum(values, -limit), limit).astype(kind)


def setup_inputs(seed: int = 0) -> dict:
    streams_of = jax.random.split(jax.random.key(seed), 12)
    token_ids = with_ends(jax.random.randint(streams_of[0], (ROWS, 2, DRAFT + 1), 0, VOCAB), jax.random.fold_in(streams_of[0], 1), 0, VOCAB - 1).astype(jnp.int32)
    accepted = with_ends(jax.random.randint(streams_of[1], (ROWS,), 0, DRAFT + 1), jax.random.fold_in(streams_of[1], 1), 0, DRAFT).astype(jnp.int32)
    lengths = with_ends(jax.random.randint(streams_of[2], (ROWS,), CTX // 4, CTX + 1), jax.random.fold_in(streams_of[2], 1), CTX // 4, CTX).astype(jnp.int32)
    queries = draw_queries(jax.random.fold_in(streams_of[11], 71), 0)
    new_kv = gaussian(streams_of[4], (ROWS, 2, 2, DRAFT + 1, KV * HD), 0.5, 4.0, ((0, 16), (4, 2)))
    cache_kv = draw_cache_kv(jax.random.fold_in(streams_of[11], 71), 0)
    table = gaussian(streams_of[6], (VOCAB, D), 1.0, 6.0, ((0, 2), (1, 16)))
    w_out = gaussian(streams_of[7], (HQ * HD, D), (HQ * HD // 4) ** -0.5, 0.1875, ((0, 2), (1, 16)))
    gain = jnp.clip(1.0 + 0.15 * jax.random.normal(streams_of[8], (D,), jnp.float32), 0.25, 1.75)
    w_feat = gaussian(streams_of[9], (D, D), D ** -0.5, 0.0625, ((0, 16), (1, 2)))
    w_emb = gaussian(streams_of[10], (D, D), D ** -0.5, 0.0625, ((0, 16), (1, 2)))
    return {"token_ids": token_ids, "accepted": accepted, "lengths": lengths, "queries": queries, "new_kv": new_kv, "cache_kv": cache_kv, "table": table, "w_out": w_out, "gain": gain, "w_feat": w_feat, "w_emb": w_emb}


def attend(queries, new_kv, cache_kv, lengths, accepted):
    steps = queries.shape[2]
    group = HQ // KV
    qv = queries.reshape(ROWS, 2, steps, KV, group, HD).astype(jnp.float32)
    keys = jnp.concatenate([cache_kv[:, 0].reshape(ROWS, CTX, KV, HD), new_kv[:, :, 0].reshape(ROWS, 2 * steps, KV, HD)], axis=1)
    vals = jnp.concatenate([cache_kv[:, 1].reshape(ROWS, CTX, KV, HD), new_kv[:, :, 1].reshape(ROWS, 2 * steps, KV, HD)], axis=1)
    scores = jnp.einsum('rtigjd,rkgd->rtigjk', qv, keys.astype(jnp.float32)) / jnp.sqrt(jnp.float32(HD))
    width = CTX + 2 * steps
    slot = jnp.arange(width, dtype=jnp.int32)[None, None, None, :]
    rnd = jnp.arange(2, dtype=jnp.int32)[None, :, None, None]
    pos = jnp.arange(steps, dtype=jnp.int32)[None, None, :, None]
    first = slot - CTX
    second = slot - CTX - steps
    seen = slot < lengths[:, None, None, None]
    seen = seen | (first >= 0) & (first < steps) & ((rnd == 0) & (first <= pos) | (rnd == 1) & (first <= accepted[:, None, None, None]))
    seen = seen | (second >= 0) & (rnd == 1) & (second <= pos)
    seen = seen[:, :, :, None, None, :]
    masked = jnp.where(seen, scores, jnp.float32(-1e+30))
    top = lax.optimization_barrier(jnp.max(masked, axis=-1, keepdims=True))
    expo = jnp.where(seen, jnp.exp(masked - top), jnp.float32(0.0))
    weights = (expo / lax.optimization_barrier(jnp.sum(expo, axis=-1, keepdims=True))).astype(jnp.bfloat16)
    out = jnp.einsum('rtigjk,rkgd->rtigjd', weights.astype(jnp.float32), vals.astype(jnp.float32))
    return out.astype(jnp.bfloat16).reshape(ROWS * 2 * steps, HQ * HD)

def reference(token_ids, accepted, lengths, queries, new_kv, cache_kv, table, w_out, gain, w_feat, w_emb):
    emb_bf = jnp.take(table, token_ids.reshape(-1), axis=0)
    emb = emb_bf.astype(jnp.float32)
    attn = attend(queries, new_kv, cache_kv, lengths, accepted)
    hidden = emb + jnp.dot(attn, w_out, preferred_element_type=jnp.float32)
    scale = jax.lax.rsqrt(lax.optimization_barrier(jnp.mean(hidden * hidden, axis=1, keepdims=True)) + 1e-05)
    feat = (hidden * scale * gain[None, :]).astype(jnp.bfloat16)
    draft = jnp.dot(feat, w_feat, preferred_element_type=jnp.float32) + jnp.dot(emb_bf, w_emb, preferred_element_type=jnp.float32)
    return (hidden.astype(jnp.bfloat16), draft.astype(jnp.bfloat16).reshape(ROWS, 2, queries.shape[2], D))
```

```python
import functools

import jax
import jax.numpy as jnp
from jax import lax
from jax.experimental import pallas as pl
from jax.experimental.pallas import tpu as pltpu
from jax.sharding import PartitionSpec as P

HD = 128
MESH = pl.DeviceIdType.MESH
VMEM_LIMIT = 60 * 1024 * 1024


def attend_kernel(steps, group, kv_heads, len_ref, acc_ref, q_ref, kv_ref, new_ref, out_ref):
    row = pl.program_id(0)
    length = len_ref[row]
    accepted = acc_ref[row]
    queries = q_ref.shape[2]
    slots = kv_ref.shape[2]
    fresh = new_ref.shape[2]
    shape = (queries, fresh)
    at = lax.broadcasted_iota(jnp.int32, shape, 0)
    new = lax.broadcasted_iota(jnp.int32, shape, 1)
    rnd = at // (steps * group)
    pos = (at // group) % steps
    seen_new = (new < steps) & (
        ((rnd == 0) & (new <= pos)) | ((rnd == 1) & (new <= accepted))
    )
    seen_new = seen_new | (
        (new >= steps) & (new < 2 * steps) & (rnd == 1) & (new - steps <= pos)
    )
    seen = lax.broadcasted_iota(jnp.int32, (queries, slots), 1) < length
    root = jnp.sqrt(jnp.float32(HD))
    low = jnp.float32(-1e30)
    rows_dot = (((1,), (1,)), ((), ()))
    for j in range(kv_heads):
        cols = slice(j * HD, (j + 1) * HD)
        q = q_ref[0, j]
        s = lax.dot_general(q, kv_ref[0, 0, :, cols], rows_dot, preferred_element_type=jnp.float32)
        sn = lax.dot_general(q, new_ref[0, 0, :, cols], rows_dot, preferred_element_type=jnp.float32)
        s = jnp.where(seen, s / root, low)
        sn = jnp.where(seen_new, sn / root, low)
        top = jnp.maximum(jnp.max(s, axis=1, keepdims=True), jnp.max(sn, axis=1, keepdims=True))
        e = jnp.where(seen, jnp.exp(s - top), 0.0)
        en = jnp.where(seen_new, jnp.exp(sn - top), 0.0)
        total = jnp.sum(e, axis=1, keepdims=True) + jnp.sum(en, axis=1, keepdims=True)
        w = (e / total).astype(jnp.bfloat16)
        wn = (en / total).astype(jnp.bfloat16)
        out = jnp.dot(w, kv_ref[0, 1, :, cols], preferred_element_type=jnp.float32)
        out = out + jnp.dot(wn, new_ref[0, 1, :, cols], preferred_element_type=jnp.float32)
        out_ref[0, j] = out.astype(jnp.bfloat16)


def attend_local(queries, new_kv, cache_kv, lengths, accepted):
    rows, _, steps, qcols = queries.shape
    slots, cols = cache_kv.shape[2:]
    kv_heads = cols // HD
    group = qcols // cols
    count = 2 * steps * group
    q = queries.reshape(rows, 2 * steps, kv_heads, group, HD)
    q = q.transpose(0, 2, 1, 3, 4).reshape(rows, kv_heads, count, HD)
    fresh = -(-2 * steps // 16) * 16
    new = new_kv.transpose(0, 2, 1, 3, 4).reshape(rows, 2, 2 * steps, cols)
    new = jnp.pad(new, ((0, 0), (0, 0), (0, fresh - 2 * steps), (0, 0)))
    out = pl.pallas_call(
        functools.partial(attend_kernel, steps, group, kv_heads),
        grid_spec=pltpu.PrefetchScalarGridSpec(
            num_scalar_prefetch=2,
            grid=(rows,),
            in_specs=[
                pl.BlockSpec((1, kv_heads, count, HD), lambda r, a, b: (r, 0, 0, 0)),
                pl.BlockSpec((1, 2, slots, cols), lambda r, a, b: (r, 0, 0, 0)),
                pl.BlockSpec((1, 2, fresh, cols), lambda r, a, b: (r, 0, 0, 0)),
            ],
            out_specs=pl.BlockSpec((1, kv_heads, count, HD), lambda r, a, b: (r, 0, 0, 0)),
        ),
        out_shape=jax.ShapeDtypeStruct((rows, kv_heads, count, HD), jnp.bfloat16),
        compiler_params=pltpu.CompilerParams(vmem_limit_bytes=VMEM_LIMIT),
        cost_estimate=pl.CostEstimate(
            flops=4 * rows * kv_heads * count * slots * HD,
            bytes_accessed=2 * cache_kv.size,
            transcendentals=rows * kv_heads * count * slots,
        ),
    )(lengths, accepted, q, cache_kv, new)
    out = out.reshape(rows, kv_heads, 2 * steps, group, HD).transpose(0, 2, 1, 3, 4)
    return out.reshape(rows * 2 * steps, qcols)


def splits(n):
    cores = 2 if n % 2 == 0 else 1
    ys = 2 if n % (2 * cores) == 0 else 1
    return cores, ys, n // (cores * ys)


def draft_kernel(
    n, width, chunks, depth_all,
    own_ref, other_ref, emb_ref, gain_ref, wf_ref, we_ref, out_ref,
    x, sq, send1, recv1, own1, send2, recv2, own2, send3, recv3, own3,
    sq_send, sq_recv, s1, r1, s2, r2, s3, r3,
):
    nc, ny, nz = splits(n)
    me = lax.axis_index("batch")
    core = me % nc
    y = (me // nc) % ny
    z = me // (nc * ny)
    share = out_ref.shape[0]
    depth = own_ref.shape[1]
    groups = nz * ny

    def hidden_of(owner):
        at = pl.ds(owner * share, share)
        proj = own_ref[at, :].astype(jnp.float32) + other_ref[at, :].astype(jnp.float32)
        return emb_ref[at, :].astype(jnp.float32) + proj

    barrier = pltpu.get_barrier_semaphore()
    for d in range(1, n):
        pl.semaphore_signal(
            barrier, inc=1, device_id={"batch": (me + d) % n}, device_id_type=MESH
        )

    ones = jnp.ones((8, depth), jnp.float32)
    everything = own_ref[...].astype(jnp.float32) + other_ref[...].astype(jnp.float32)
    everything = emb_ref[...].astype(jnp.float32) + everything
    squares = lax.dot_general(
        ones, everything * everything, (((1,), (1,)), ((), ())),
        preferred_element_type=jnp.float32, precision=lax.Precision.HIGHEST,
    )
    sq[me] = squares[:1]
    pl.semaphore_wait(barrier, n - 1)

    copies = []
    for d in range(1, n):
        copy = pltpu.make_async_remote_copy(
            src_ref=sq.at[me], dst_ref=sq.at[me],
            send_sem=sq_send.at[d], recv_sem=sq_recv.at[d],
            device_id={"batch": (me + d) % n}, device_id_type=MESH,
        )
        copy.start()
        copies.append(copy)
    for copy in copies:
        copy.wait()

    total = sq[0]
    for d in range(1, n):
        total = total + sq[d]
    total = jnp.broadcast_to(total, (8, total.shape[1]))
    scale = lax.rsqrt(total / depth_all + 1e-05)
    column = jnp.transpose(scale)[:, :1]
    for owner in range(n):
        at = slice(owner * share, (owner + 1) * share)
        place = slice((owner // nc) * share, (owner // nc + 1) * share)
        feat = hidden_of(owner) * column[at] * gain_ref[...]
        x[owner % nc, place, :depth] = feat.astype(jnp.bfloat16)
        x[owner % nc, place, depth:] = emb_ref[at, :]

    def product(t, which):
        cols = pl.ds(pl.multiple_of(t * width, width), width)
        rows = x[which]
        out = jnp.dot(rows[:, :depth], wf_ref[:, cols], preferred_element_type=jnp.float32)
        return out + jnp.dot(rows[:, depth:], we_ref[:, cols], preferred_element_type=jnp.float32)

    def core_copy(t):
        return pltpu.make_async_remote_copy(
            src_ref=send1.at[t], dst_ref=recv1.at[t], send_sem=s1.at[t], recv_sem=r1.at[t],
            device_id={"batch": me + 1 - 2 * core}, device_id_type=MESH,
        )

    def y_copy(t):
        return pltpu.make_async_remote_copy(
            src_ref=send2.at[t], dst_ref=recv2.at[t], send_sem=s2.at[t], recv_sem=r2.at[t],
            device_id={"batch": me + nc * (1 - 2 * y)}, device_id_type=MESH,
        )

    def z_copy(t, d):
        to = (z + d) % nz
        return pltpu.make_async_remote_copy(
            src_ref=send3.at[t, to], dst_ref=recv3.at[t, d], send_sem=s3.at[t, d],
            recv_sem=r3.at[t, d],
            device_id={"batch": to * (nc * ny) + me % (nc * ny)}, device_id_type=MESH,
        )

    def stage_product(t):
        if nc > 1:
            send1[t] = product(t, 1 - core).astype(jnp.bfloat16).reshape(groups, share, width)
            core_copy(t).start()
        own1[t % 2] = product(t, core).reshape(groups, share, width)

    def stage_core(t):
        if nc > 1:
            core_copy(t).wait()
        for k in range(nz):
            for v in ([1, 0] if ny > 1 else [0]):
                which = (y + v) % ny
                g = k * ny + which
                value = own1[t % 2, g]
                if nc > 1:
                    value = value + recv1[t, g].astype(jnp.float32)
                if v:
                    send2[t, k] = value.astype(jnp.bfloat16)
                else:
                    own2[t % 2, k] = value
        if ny > 1:
            y_copy(t).start()

    def stage_y(t):
        if ny > 1:
            y_copy(t).wait()
        for d in range(nz):
            to = (z + d) % nz
            value = own2[t % 2, to]
            if ny > 1:
                value = value + recv2[t, to].astype(jnp.float32)
            if d:
                send3[t, to] = value.astype(jnp.bfloat16)
                z_copy(t, d).start()
            else:
                own3[t % 2] = value

    def stage_z(t):
        value = own3[t % 2]
        for d in range(1, nz):
            z_copy(t, d).wait()
            value = value + recv3[t, d].astype(jnp.float32)
        cols = pl.ds(pl.multiple_of(t * width, width), width)
        out_ref[:, cols] = value.astype(out_ref.dtype)

    def step(t, carry):
        @pl.when(t < chunks)
        def _():
            stage_product(t)

        @pl.when((t >= 1) & (t < chunks + 1))
        def _():
            stage_core(t - 1)

        @pl.when((t >= 2) & (t < chunks + 2))
        def _():
            stage_y(t - 2)

        @pl.when(t >= 3)
        def _():
            stage_z(t - 3)

        return carry

    lax.fori_loop(0, chunks + 3, step, 0)


def draft_local(own, other, emb, gain, w_feat, w_emb, n):
    total_rows, depth = own.shape
    out_cols = w_feat.shape[1]
    share = total_rows // n
    nc, ny, nz = splits(n)
    width = 512
    while out_cols % width:
        width //= 2
    chunks = out_cols // width
    groups = ny * nz
    bf, f32 = jnp.bfloat16, jnp.float32
    dma = pltpu.SemaphoreType.DMA
    vmem = pl.BlockSpec(memory_space=pltpu.VMEM)
    return pl.pallas_call(
        functools.partial(draft_kernel, n, width, chunks, depth * n),
        out_shape=jax.ShapeDtypeStruct((share, out_cols), bf),
        in_specs=[vmem] * 6,
        out_specs=vmem,
        scratch_shapes=[
            pltpu.VMEM((nc, total_rows // nc, 2 * depth), bf),
            pltpu.VMEM((n, 1, total_rows), f32),
            pltpu.VMEM((chunks, groups, share, width), bf),
            pltpu.VMEM((chunks, groups, share, width), bf),
            pltpu.VMEM((2, groups, share, width), f32),
            pltpu.VMEM((chunks, nz, share, width), bf),
            pltpu.VMEM((chunks, nz, share, width), bf),
            pltpu.VMEM((2, nz, share, width), f32),
            pltpu.VMEM((chunks, nz, share, width), bf),
            pltpu.VMEM((chunks, nz, share, width), bf),
            pltpu.VMEM((2, share, width), f32),
            dma((n,)),
            dma((n,)),
            dma((chunks,)),
            dma((chunks,)),
            dma((chunks,)),
            dma((chunks,)),
            dma((chunks, nz)),
            dma((chunks, nz)),
        ],
        compiler_params=pltpu.CompilerParams(
            collective_id=0, has_side_effects=True, vmem_limit_bytes=VMEM_LIMIT
        ),
        cost_estimate=pl.CostEstimate(
            flops=4 * total_rows * depth * out_cols,
            bytes_accessed=4 * depth * out_cols,
            transcendentals=0,
        ),
    )(own, other, emb, gain.reshape(1, depth), w_feat, w_emb)


def swap(value):
    return lax.ppermute(value, "heads", [(0, 1), (1, 0)])


def body(
    n, nh,
    token_ids, accepted, lengths, queries, new_kv, cache_kv, table, w_out, gain, w_feat, w_emb
):
    rows, _, steps = token_ids.shape
    all_ids = lax.all_gather(token_ids.reshape(-1), "batch", axis=0, tiled=True)
    vocab_rows = table.shape[0]
    base = lax.axis_index("heads") * vocab_rows
    local_ids = all_ids - base
    inside = (local_ids >= 0) & (local_ids < vocab_rows)
    picked = jnp.take(table, jnp.clip(local_ids, 0, vocab_rows - 1), axis=0)
    partial_emb = jnp.where(inside[:, None], picked, jnp.bfloat16(0.0))
    if nh == 2:
        emb = jnp.where(inside[:, None], picked, swap(partial_emb))
    else:
        emb = lax.psum(partial_emb, "heads")
    attn = attend_local(queries, new_kv, cache_kv, lengths, accepted)
    proj = jnp.dot(
        lax.all_gather(attn, "batch", axis=0, tiled=True), w_out, preferred_element_type=jnp.float32
    )
    if nh == 2:
        own = proj.astype(jnp.bfloat16)
        other = swap(own)
    else:
        proj = lax.psum(proj, "heads")
        own = proj.astype(jnp.bfloat16)
        other = (proj - own.astype(jnp.float32)).astype(jnp.bfloat16)
    hidden = emb.astype(jnp.float32) + (own.astype(jnp.float32) + other.astype(jnp.float32))
    draft = draft_local(own, other, emb, gain, w_feat, w_emb, n)
    return (hidden.astype(jnp.bfloat16), draft.reshape(rows, 2, steps, w_feat.shape[1]))


def solution(mesh):
    placed = (
        P("batch", None, None),
        P("batch"),
        P("batch"),
        P("batch", None, None, "heads"),
        P("batch", None, None, None, "heads"),
        P("batch", None, None, "heads"),
        P("heads", "batch"),
        P("heads", "batch"),
        P("batch"),
        P("batch", "heads"),
        P("batch", "heads"),
    )
    return jax.shard_map(
        functools.partial(body, mesh.shape["batch"], mesh.shape["heads"]),
        mesh=mesh,
        in_specs=placed,
        out_specs=(P(None, "batch"), P("batch", None, None, "heads")),
        check_vma=False,
    )
```

```python
import functools

import jax
import jax.numpy as jnp
from jax import lax
from jax.experimental import pallas as pl
from jax.experimental.pallas import tpu as pltpu
from jax.sharding import PartitionSpec as P

HD = 128
MESH = pl.DeviceIdType.MESH
VMEM_LIMIT = 60 * 1024 * 1024


def attend_kernel(steps, group, kv_heads, len_ref, acc_ref, q_ref, kv_ref, new_ref, out_ref):
    row = pl.program_id(0)
    length = len_ref[row]
    accepted = acc_ref[row]
    queries = q_ref.shape[2]
    slots = kv_ref.shape[2]
    fresh = new_ref.shape[2]
    shape = (queries, fresh)
    at = lax.broadcasted_iota(jnp.int32, shape, 0)
    new = lax.broadcasted_iota(jnp.int32, shape, 1)
    rnd = at // (steps * group)
    pos = (at // group) % steps
    seen_new = (new < steps) & (
        ((rnd == 0) & (new <= pos)) | ((rnd == 1) & (new <= accepted))
    )
    seen_new = seen_new | (
        (new >= steps) & (new < 2 * steps) & (rnd == 1) & (new - steps <= pos)
    )
    seen = lax.broadcasted_iota(jnp.int32, (queries, slots), 1) < length
    root = jnp.sqrt(jnp.float32(HD))
    low = jnp.float32(-1e30)
    rows_dot = (((1,), (1,)), ((), ()))
    for j in range(kv_heads):
        cols = slice(j * HD, (j + 1) * HD)
        q = q_ref[0, j]
        s = lax.dot_general(q, kv_ref[0, 0, :, cols], rows_dot, preferred_element_type=jnp.float32)
        sn = lax.dot_general(q, new_ref[0, 0, :, cols], rows_dot, preferred_element_type=jnp.float32)
        s = jnp.where(seen, s / root, low)
        sn = jnp.where(seen_new, sn / root, low)
        top = jnp.maximum(jnp.max(s, axis=1, keepdims=True), jnp.max(sn, axis=1, keepdims=True))
        e = jnp.where(seen, jnp.exp(s - top), 0.0)
        en = jnp.where(seen_new, jnp.exp(sn - top), 0.0)
        total = jnp.sum(e, axis=1, keepdims=True) + jnp.sum(en, axis=1, keepdims=True)
        w = (e / total).astype(jnp.bfloat16)
        wn = (en / total).astype(jnp.bfloat16)
        out = jnp.dot(w, kv_ref[0, 1, :, cols], preferred_element_type=jnp.float32)
        out = out + jnp.dot(wn, new_ref[0, 1, :, cols], preferred_element_type=jnp.float32)
        out_ref[0, j] = out.astype(jnp.bfloat16)


def attend_local(queries, new_kv, cache_kv, lengths, accepted):
    rows, _, steps, qcols = queries.shape
    slots, cols = cache_kv.shape[2:]
    kv_heads = cols // HD
    group = qcols // cols
    count = 2 * steps * group
    q = queries.reshape(rows, 2 * steps, kv_heads, group, HD)
    q = q.transpose(0, 2, 1, 3, 4).reshape(rows, kv_heads, count, HD)
    fresh = -(-2 * steps // 16) * 16
    new = new_kv.transpose(0, 2, 1, 3, 4).reshape(rows, 2, 2 * steps, cols)
    new = jnp.pad(new, ((0, 0), (0, 0), (0, fresh - 2 * steps), (0, 0)))
    out = pl.pallas_call(
        functools.partial(attend_kernel, steps, group, kv_heads),
        grid_spec=pltpu.PrefetchScalarGridSpec(
            num_scalar_prefetch=2,
            grid=(rows,),
            in_specs=[
                pl.BlockSpec((1, kv_heads, count, HD), lambda r, a, b: (r, 0, 0, 0)),
                pl.BlockSpec((1, 2, slots, cols), lambda r, a, b: (r, 0, 0, 0)),
                pl.BlockSpec((1, 2, fresh, cols), lambda r, a, b: (r, 0, 0, 0)),
            ],
            out_specs=pl.BlockSpec((1, kv_heads, count, HD), lambda r, a, b: (r, 0, 0, 0)),
        ),
        out_shape=jax.ShapeDtypeStruct((rows, kv_heads, count, HD), jnp.bfloat16),
        compiler_params=pltpu.CompilerParams(vmem_limit_bytes=VMEM_LIMIT),
        cost_estimate=pl.CostEstimate(
            flops=4 * rows * kv_heads * count * slots * HD,
            bytes_accessed=2 * cache_kv.size,
            transcendentals=rows * kv_heads * count * slots,
        ),
    )(lengths, accepted, q, cache_kv, new)
    out = out.reshape(rows, kv_heads, 2 * steps, group, HD).transpose(0, 2, 1, 3, 4)
    return out.reshape(rows * 2 * steps, qcols)


def splits(n):
    cores = 2 if n % 2 == 0 else 1
    ys = 2 if n % (2 * cores) == 0 else 1
    return cores, ys, n // (cores * ys)


def gather_project(
    n, attn_ref, emb1_ref, emb2_ref, wo_ref, own, other, emb, landed, gat,
    zs, zr, ys, yr, cs, cr, xs, xr, es, er,
):
    nc, ny, nz = splits(n)
    me = lax.axis_index("batch")
    head = lax.axis_index("heads")
    core = me % nc
    y = (me // nc) % ny
    z = me // (nc * ny)
    group = nc * ny
    rows = attn_ref.shape[0] * group
    sign = 1 - 2 * ((2 * z) // nz)

    emb_copy = pltpu.make_async_remote_copy(
        src_ref=emb2_ref, dst_ref=landed, send_sem=es, recv_sem=er,
        device_id={"heads": 1 - head}, device_id_type=MESH,
    )
    emb_copy.start()
    gat[me] = attn_ref[...]

    def z_copy(block, way, to):
        at = block * group + me % group
        return pltpu.make_async_remote_copy(
            src_ref=gat.at[at], dst_ref=gat.at[at],
            send_sem=zs.at[way, block], recv_sem=zr.at[way, block],
            device_id={"batch": to * group + me % group}, device_id_type=MESH,
        )

    def y_copy(block):
        at = block * group + me % group
        return pltpu.make_async_remote_copy(
            src_ref=gat.at[at], dst_ref=gat.at[at], send_sem=ys.at[block], recv_sem=yr.at[block],
            device_id={"batch": me + nc * (1 - 2 * y)}, device_id_type=MESH,
        )

    def core_copy(block, line):
        at = block * group + line * nc + core
        return pltpu.make_async_remote_copy(
            src_ref=gat.at[at], dst_ref=gat.at[at],
            send_sem=cs.at[block, line], recv_sem=cr.at[block, line],
            device_id={"batch": me + 1 - 2 * core}, device_id_type=MESH,
        )

    def x_copy(block):
        at = pl.ds(pl.multiple_of(block * rows, 16), rows)
        return pltpu.make_async_remote_copy(
            src_ref=own.at[at], dst_ref=other.at[at], send_sem=xs.at[block], recv_sem=xr.at[block],
            device_id={"heads": 1 - head}, device_id_type=MESH,
        )

    def spread(block):
        if ny > 1:
            y_copy(block).start()
        if nc > 1:
            core_copy(block, y).start()

    def finish(i):
        block = (z + sign * i + nz) % nz
        if ny > 1:
            y_copy(block).wait()
            if nc > 1:
                core_copy(block, 1 - y).start()
        if nc > 1:
            for line in range(ny):
                core_copy(block, line).wait()
        value = gat[pl.ds(block * group, group)].reshape(rows, gat.shape[2])
        value = jnp.dot(value, wo_ref[...], preferred_element_type=jnp.float32)
        own[pl.ds(pl.multiple_of(block * rows, 16), rows), :] = value.astype(own.dtype)
        x_copy(block).start()

    @pl.when(z < nz - 1)
    def _():
        z_copy(z, 0, z + 1).start()

    @pl.when(z > 0)
    def _():
        z_copy(z, 1, z - 1).start()

    spread(z)
    for s in range(1, nz):
        @pl.when(z >= s)
        def _():
            z_copy(z - s, 0, z).wait_recv()

            @pl.when(z < nz - 1)
            def _():
                z_copy(z - s, 0, z + 1).start()

            spread(z - s)

        @pl.when(z + s < nz)
        def _():
            z_copy(z + s, 1, z).wait_recv()

            @pl.when(z > 0)
            def _():
                z_copy(z + s, 1, z - 1).start()

            spread(z + s)

        finish(s - 1)
    finish(nz - 1)

    for s in range(nz):
        @pl.when((z >= s) & (z < nz - 1))
        def _():
            z_copy(z - s, 0, z + 1).wait_send()

        @pl.when((z + s < nz) & (z > 0))
        def _():
            z_copy(z + s, 1, z - 1).wait_send()

    emb_copy.wait()
    half = emb1_ref.shape[0]
    emb[:half, :] = emb1_ref[...]
    emb[half:, :] = emb2_ref[...] + landed[...]
    for i in range(nz):
        x_copy((z + sign * i + nz) % nz).wait()


def greet(n, both):
    me = lax.axis_index("batch")
    barrier = pltpu.get_barrier_semaphore()
    for d in range(1, n):
        pl.semaphore_signal(
            barrier, inc=1, device_id={"batch": (me + d) % n}, device_id_type=MESH
        )
    if both:
        pl.semaphore_signal(
            barrier, inc=1, device_id={"heads": 1 - lax.axis_index("heads")}, device_id_type=MESH
        )
    pl.semaphore_wait(barrier, n - 1 + both)


def fused_kernel(n, width, chunks, depth_all, *refs):
    attn, emb1, emb2, gain, wo, wf, we = refs[:7]
    out, hid = refs[7:9]
    front = refs[9:24]
    own, other, emb = front[:3]
    wf_in, we_in, w_sem = refs[24:27]
    rest = refs[27:]
    loads = [
        pltpu.make_async_copy(wf, wf_in, w_sem.at[0]),
        pltpu.make_async_copy(we, we_in, w_sem.at[1]),
    ]
    for load in loads:
        load.start()
    greet(n, 1)
    gather_project(n, attn, emb1, emb2, wo, *front)
    for load in loads:
        load.wait()
    draft(n, width, chunks, depth_all, own, other, emb, gain, wf_in, we_in, out, hid, *rest)


def draft_kernel(n, width, chunks, depth_all, *refs):
    greet(n, 0)
    draft(n, width, chunks, depth_all, *refs)


def draft(
    n, width, chunks, depth_all,
    own_ref, other_ref, emb_ref, gain_ref, wf_ref, we_ref, out_ref, hid_ref,
    x, sq, send1, recv1, own1, send2, recv2, own2, send3, recv3, own3,
    sq_send, sq_recv, s1, r1, s2, r2, s3, r3,
):
    nc, ny, nz = splits(n)
    me = lax.axis_index("batch")
    core = me % nc
    y = (me // nc) % ny
    z = me // (nc * ny)
    share = out_ref.shape[0]
    depth = own_ref.shape[1]
    groups = nz * ny

    def hidden_of(owner):
        at = pl.ds(owner * share, share)
        proj = own_ref[at, :].astype(jnp.float32) + other_ref[at, :].astype(jnp.float32)
        return emb_ref[at, :].astype(jnp.float32) + proj

    ones = jnp.ones((8, depth), jnp.float32)
    everything = own_ref[...].astype(jnp.float32) + other_ref[...].astype(jnp.float32)
    everything = emb_ref[...].astype(jnp.float32) + everything
    squares = lax.dot_general(
        ones, everything * everything, (((1,), (1,)), ((), ())),
        preferred_element_type=jnp.float32, precision=lax.Precision.HIGHEST,
    )
    sq[me] = squares[:1]

    copies = []
    for d in range(1, n):
        copy = pltpu.make_async_remote_copy(
            src_ref=sq.at[me], dst_ref=sq.at[me],
            send_sem=sq_send.at[d], recv_sem=sq_recv.at[d],
            device_id={"batch": (me + d) % n}, device_id_type=MESH,
        )
        copy.start()
        copies.append(copy)
    for copy in copies:
        copy.wait()

    total = sq[0]
    for d in range(1, n):
        total = total + sq[d]
    total = jnp.broadcast_to(total, (8, total.shape[1]))
    scale = lax.rsqrt(total / depth_all + 1e-05)
    column = jnp.transpose(scale)[:, :1]
    for owner in range(n):
        at = slice(owner * share, (owner + 1) * share)
        place = slice((owner // nc) * share, (owner // nc + 1) * share)
        hidden = hidden_of(owner)
        hid_ref[at, :] = hidden.astype(hid_ref.dtype)
        feat = hidden * column[at] * gain_ref[...]
        x[owner % nc, place, :depth] = feat.astype(jnp.bfloat16)
        x[owner % nc, place, depth:] = emb_ref[at, :]

    def product(t, which):
        cols = pl.ds(pl.multiple_of(t * width, width), width)
        rows = x[which]
        out = jnp.dot(rows[:, :depth], wf_ref[:, cols], preferred_element_type=jnp.float32)
        return out + jnp.dot(rows[:, depth:], we_ref[:, cols], preferred_element_type=jnp.float32)

    def core_copy(t):
        return pltpu.make_async_remote_copy(
            src_ref=send1.at[t], dst_ref=recv1.at[t], send_sem=s1.at[t], recv_sem=r1.at[t],
            device_id={"batch": me + 1 - 2 * core}, device_id_type=MESH,
        )

    def y_copy(t):
        return pltpu.make_async_remote_copy(
            src_ref=send2.at[t], dst_ref=recv2.at[t], send_sem=s2.at[t], recv_sem=r2.at[t],
            device_id={"batch": me + nc * (1 - 2 * y)}, device_id_type=MESH,
        )

    def z_copy(t, d):
        to = (z + d) % nz
        return pltpu.make_async_remote_copy(
            src_ref=send3.at[t, to], dst_ref=recv3.at[t, d], send_sem=s3.at[t, d],
            recv_sem=r3.at[t, d],
            device_id={"batch": to * (nc * ny) + me % (nc * ny)}, device_id_type=MESH,
        )

    def stage_product(t):
        if nc > 1:
            send1[t] = product(t, 1 - core).astype(jnp.bfloat16).reshape(groups, share, width)
            core_copy(t).start()
        own1[t % 2] = product(t, core).reshape(groups, share, width)

    def stage_core(t):
        if nc > 1:
            core_copy(t).wait()
        for k in range(nz):
            for v in ([1, 0] if ny > 1 else [0]):
                which = (y + v) % ny
                g = k * ny + which
                value = own1[t % 2, g]
                if nc > 1:
                    value = value + recv1[t, g].astype(jnp.float32)
                if v:
                    send2[t, k] = value.astype(jnp.bfloat16)
                else:
                    own2[t % 2, k] = value
        if ny > 1:
            y_copy(t).start()

    def stage_y(t):
        if ny > 1:
            y_copy(t).wait()
        for d in range(nz):
            to = (z + d) % nz
            value = own2[t % 2, to]
            if ny > 1:
                value = value + recv2[t, to].astype(jnp.float32)
            if d:
                send3[t, to] = value.astype(jnp.bfloat16)
                z_copy(t, d).start()
            else:
                own3[t % 2] = value

    def stage_z(t):
        value = own3[t % 2]
        for d in range(1, nz):
            z_copy(t, d).wait()
            value = value + recv3[t, d].astype(jnp.float32)
        cols = pl.ds(pl.multiple_of(t * width, width), width)
        out_ref[:, cols] = value.astype(out_ref.dtype)

    def step(t, carry):
        @pl.when(t < chunks)
        def _():
            stage_product(t)

        @pl.when((t >= 1) & (t < chunks + 1))
        def _():
            stage_core(t - 1)

        @pl.when((t >= 2) & (t < chunks + 2))
        def _():
            stage_y(t - 2)

        @pl.when(t >= 3)
        def _():
            stage_z(t - 3)

        return carry

    lax.fori_loop(0, chunks + 3, step, 0)


def draft_local(front, gain, w_feat, w_emb, n, w_out=None):
    depth, out_cols = w_feat.shape
    fused = w_out is not None
    share = front[0].shape[0] if fused else front[0].shape[0] // n
    total_rows = share * n
    nc, ny, nz = splits(n)
    width = 256
    while out_cols % width:
        width //= 2
    chunks = out_cols // width
    groups = ny * nz
    bf, f32 = jnp.bfloat16, jnp.float32
    dma = pltpu.SemaphoreType.DMA
    vmem = pl.BlockSpec(memory_space=pltpu.VMEM)
    hbm = pl.BlockSpec(memory_space=pl.ANY)
    scratch = [
        pltpu.VMEM((nc, total_rows // nc, 2 * depth), bf),
        pltpu.VMEM((n, 1, total_rows), f32),
        pltpu.VMEM((chunks, groups, share, width), bf),
        pltpu.VMEM((chunks, groups, share, width), bf),
        pltpu.VMEM((2, groups, share, width), f32),
        pltpu.VMEM((chunks, nz, share, width), bf),
        pltpu.VMEM((chunks, nz, share, width), bf),
        pltpu.VMEM((2, nz, share, width), f32),
        pltpu.VMEM((chunks, nz, share, width), bf),
        pltpu.VMEM((chunks, nz, share, width), bf),
        pltpu.VMEM((2, share, width), f32),
        dma((n,)),
        dma((n,)),
        dma((chunks,)),
        dma((chunks,)),
        dma((chunks,)),
        dma((chunks,)),
        dma((chunks, nz)),
        dma((chunks, nz)),
    ]
    gain = gain.reshape(1, depth)
    if fused:
        half = front[2].shape[0]
        whole = pltpu.VMEM((total_rows, depth), bf)
        scratch = [
            whole,
            whole,
            whole,
            pltpu.VMEM((half, depth), bf),
            pltpu.VMEM((n, share, w_out.shape[0]), bf),
            dma((2, nz)),
            dma((2, nz)),
            dma((nz,)),
            dma((nz,)),
            dma((nz, ny)),
            dma((nz, ny)),
            dma((nz,)),
            dma((nz,)),
            dma,
            dma,
            pltpu.VMEM(w_feat.shape, bf),
            pltpu.VMEM(w_emb.shape, bf),
            dma((2,)),
        ] + scratch
        args = (*front, gain, w_out, w_feat, w_emb)
        specs = [vmem] * 5 + [hbm] * 2
    else:
        args = (*front, gain, w_feat, w_emb)
        specs = [vmem] * 6
    return pl.pallas_call(
        functools.partial(
            fused_kernel if fused else draft_kernel, n, width, chunks, depth * n
        ),
        out_shape=(
            jax.ShapeDtypeStruct((share, out_cols), bf),
            jax.ShapeDtypeStruct((total_rows, depth), bf),
        ),
        in_specs=specs,
        out_specs=(vmem, vmem),
        scratch_shapes=scratch,
        compiler_params=pltpu.CompilerParams(
            collective_id=0, has_side_effects=True, vmem_limit_bytes=VMEM_LIMIT
        ),
        cost_estimate=pl.CostEstimate(
            flops=4 * total_rows * depth * out_cols,
            bytes_accessed=4 * depth * out_cols,
            transcendentals=0,
        ),
    )(*args)


def swap(value):
    return lax.ppermute(value, "heads", [(0, 1), (1, 0)])


def body(
    n, nh,
    token_ids, accepted, lengths, queries, new_kv, cache_kv, table, w_out, gain, w_feat, w_emb
):
    rows, _, steps = token_ids.shape
    share = rows * 2 * steps
    lanes = -(-share // 128) * 128
    ids = jnp.pad(token_ids.reshape(1, share), ((0, 7), (0, lanes - share)))
    all_ids = lax.all_gather(ids, "batch", axis=0, tiled=True)
    all_ids = all_ids.reshape(n, 8, lanes)[:, 0, :share].reshape(-1)
    vocab_rows = table.shape[0]
    base = lax.axis_index("heads") * vocab_rows

    def lookup(some):
        local_ids = some - base
        inside = (local_ids >= 0) & (local_ids < vocab_rows)
        picked = jnp.take(table, jnp.clip(local_ids, 0, vocab_rows - 1), axis=0)
        return jnp.where(inside[:, None], picked, jnp.bfloat16(0.0))

    attn = attend_local(queries, new_kv, cache_kv, lengths, accepted)
    if nh == 2:
        half = n * share // 2
        first = lookup(all_ids[:half])
        held = swap(first)
        first_emb = first + held
        later, first = lax.optimization_barrier((all_ids[half:], first))
        second = lookup(later)
        draft, hidden = draft_local(
            (attn, first_emb, second), gain, w_feat, w_emb, n, w_out
        )
    else:
        emb = lax.psum(lookup(all_ids), "heads")
        proj = jnp.dot(
            lax.all_gather(attn, "batch", axis=0, tiled=True),
            w_out,
            preferred_element_type=jnp.float32,
        )
        proj = lax.psum(proj, "heads")
        own = proj.astype(jnp.bfloat16)
        other = (proj - own.astype(jnp.float32)).astype(jnp.bfloat16)
        draft, hidden = draft_local((own, other, emb), gain, w_feat, w_emb, n)
    return (hidden, draft.reshape(rows, 2, steps, w_feat.shape[1]))


def solution(mesh):
    placed = (
        P("batch", None, None),
        P("batch"),
        P("batch"),
        P("batch", None, None, "heads"),
        P("batch", None, None, None, "heads"),
        P("batch", None, None, "heads"),
        P("heads", "batch"),
        P("heads", "batch"),
        P("batch"),
        P("batch", "heads"),
        P("batch", "heads"),
    )
    return jax.shard_map(
        functools.partial(body, mesh.shape["batch"], mesh.shape["heads"]),
        mesh=mesh,
        in_specs=placed,
        out_specs=(P(None, "batch"), P("batch", None, None, "heads")),
        check_vma=False,
    )
```
